512 devices in a mesh: replica: 64 (over y, z), tensor: 8 (over x, core).
Axes of the slice: x: 4, y: 4, z: 16, core: 2. Of those that a mesh axis runs over, the one named last changes fastest.
Arguments:
- qkv_grads: float32 [64, 64, 18432], P('replica', None, 'tensor'), may hold values from -65 to 65
- proj_grads: float32 [64, 64, 6144], P('replica', None, 'tensor'), may hold values from -65 to 65
- mlp_in_grads: float32 [64, 64, 24576], P('replica', None, 'tensor'), may hold values from -65 to 65
- mlp_out_grads: float32 [64, 64, 24576], P('replica', None, 'tensor'), may hold values from -65 to 65
Outputs:
- qkv_combined: float32 [64, 18432], P('replica', 'tensor')
- proj_combined: float32 [64, 6144], P('replica', 'tensor')
- mlp_in_combined: float32 [64, 24576], P('replica', 'tensor')
- mlp_out_combined: float32 [64, 24576], P('replica', 'tensor')
The draws below stay inside these ranges and needn't reach their ends.
All inputs are finite; a program needn't handle non-finite values.
Results may differ from the reference program's by a relative error of at most 0.00011.
Values sent between devices are 32-bit elements; how exact they have to be, the bound alone decides.
A program may use at most 64 MiB of HBM per device.

```python
import math
import jax
import jax.numpy as jnp

D = 6144
FF = 24576
ROWS = 64
REPLICAS = 64


def shape_gradient(key, common, own, share_low, share_high, column_top):
    keys = jax.random.split(key, 4)
    cols = common.shape[1]
    rising = 3.0 ** (jnp.arange(REPLICAS, dtype=jnp.float32) / (REPLICAS - 1))
    replica_scale = rising * jax.random.uniform(keys[0], (REPLICAS,), minval=0.8, maxval=1.25)
    shares = jax.random.uniform(keys[1], (REPLICAS,), minval=share_low, maxval=share_high)
    row_scale = jnp.exp(jax.random.uniform(keys[2], (ROWS,), minval=math.log(0.3), maxval=math.log(3.0)))
    col_scale = jnp.exp(jax.random.uniform(keys[3], (cols,), minval=math.log(0.3), maxval=math.log(0.3 * column_top)))
    mixed = shares[:, None, None] * common[None] + (1.0 - shares[:, None, None]) * own
    return 0.3 * replica_scale[:, None, None] * mixed * row_scale[None, :, None] * col_scale[None, None, :]


def draw_qkv_grads(key, part):
    key = jax.random.fold_in(key, 11)
    keys = jax.random.split(key, 3)
    cols = 3 * D
    common = jnp.clip(jax.random.normal(keys[0], (ROWS, cols)), -4.0, 4.0)
    own = jnp.clip(jax.random.normal(keys[1], (REPLICAS, ROWS, cols)), -4.0, 4.0)
    return shape_gradient(keys[2], common, own, 0.3, 0.9, 10.0)


def draw_proj_grads(key, part):
    key = jax.random.fold_in(key, 23)
    keys = jax.random.split(key, 3)
    cols = D
    common = jnp.clip(jax.random.normal(keys[0], (ROWS, cols)), -4.0, 4.0)
    own = jnp.clip(jax.random.normal(keys[1], (REPLICAS, ROWS, cols)), -4.0, 4.0)
    return shape_gradient(keys[2], common, own, 0.3, 0.9, 10.0)


def draw_mlp_in_grads(key, part):
    key = jax.random.fold_in(key, 37)
    keys = jax.random.split(key, 3)
    cols = FF
    common = jnp.clip(jax.random.normal(keys[0], (ROWS, cols)), -4.0, 4.0)
    own = jnp.clip(jax.random.normal(keys[1], (REPLICAS, ROWS, cols)), -4.0, 4.0)
    return shape_gradient(keys[2], common, own, 0.3, 0.9, 10.0)


def draw_mlp_out_grads(key, part):
    key = jax.random.fold_in(key, 41)
    keys = jax.random.split(key, 3)
    cols = FF
    common = jnp.clip(jax.random.normal(keys[0], (ROWS, cols)), -4.0, 4.0)
    own = jnp.clip(jax.random.normal(keys[1], (REPLICAS, ROWS, cols)), -4.0, 4.0)
    return shape_gradient(keys[2], common, own, 0.3, 0.9, 10.0)


def setup_inputs(seed: int = 0) -> dict:
    key_of = jax.random.split(jax.random.key(seed), 5)
    return {
        "qkv_grads": draw_qkv_grads(jax.random.fold_in(key_of[4], 71), 0),
        "proj_grads": draw_proj_grads(jax.random.fold_in(key_of[4], 71), 0),
        "mlp_in_grads": draw_mlp_in_grads(jax.random.fold_in(key_of[4], 71), 0),
        "mlp_out_grads": draw_mlp_out_grads(jax.random.fold_in(key_of[4], 71), 0),
    }


def adasum_tree(grads):
    current = grads.astype(jnp.float32)
    sections = REPLICAS.bit_length() - 1
    for section_bit in range(sections):
        pairs = current.reshape(current.shape[0] // 2, 2, current.shape[1], current.shape[2])
        lower_group = pairs[:, 0]
        upper_group = pairs[:, 1]
        cross = jnp.sum(lower_group * upper_group, axis=(1, 2))[:, None, None]
        lower_norm = jnp.sum(lower_group * lower_group, axis=(1, 2))[:, None, None] + 1e-6
        upper_norm = jnp.sum(upper_group * upper_group, axis=(1, 2))[:, None, None] + 1e-6
        current = (1.0 - cross / (2.0 * lower_norm)) * lower_group + (1.0 - cross / (2.0 * upper_norm)) * upper_group
    return current[0]


def reference(qkv_grads, proj_grads, mlp_in_grads, mlp_out_grads):
    return (adasum_tree(qkv_grads), adasum_tree(proj_grads), adasum_tree(mlp_in_grads), adasum_tree(mlp_out_grads))
```

```python
import functools

import jax
import jax.numpy as jnp
from jax import lax
from jax.experimental import pallas as pl
from jax.experimental.pallas import tpu as pltpu
from jax.sharding import PartitionSpec as P

EPSILON = 1e-06
LANES = 128
TRUSTED = 0.03
MESH = pl.DeviceIdType.MESH


def lower_weight(cross, norm):
    return 1.0 - cross / (2.0 * (norm + EPSILON))


def tree_weights(gram):
    count = gram.shape[0]
    across = lax.broadcasted_iota(jnp.int32, (count, count), 1)
    down = lax.broadcasted_iota(jnp.int32, (count, count), 0)
    coefficients = jnp.ones((count, 1), jnp.float32)
    doubtful = jnp.zeros((count, 1), jnp.float32)
    scaled = gram
    for level in range(count.bit_length() - 1):
        same = (across >> level) == (down >> level)
        either = (across >> (level + 1)) == (down >> (level + 1))
        own = jnp.where(same, scaled, 0.0)
        sibling = jnp.where(either, scaled, 0.0) - own
        sizes = jnp.abs(own)

        def column_of(terms):
            partial = jnp.sum(terms, axis=0, keepdims=True)
            return jnp.sum(jnp.where(same, partial, 0.0), axis=1, keepdims=True)

        def row_of(terms):
            partial = jnp.sum(terms, axis=1, keepdims=True)
            return jnp.sum(jnp.where(same, partial, 0.0), axis=0, keepdims=True)

        norm = column_of(own)
        column = lower_weight(column_of(sibling), norm)
        row = lower_weight(row_of(sibling), row_of(own))
        doubtful = jnp.maximum(
            doubtful, jnp.where(norm < TRUSTED * column_of(sizes), 1.0, 0.0)
        )
        coefficients = coefficients * column
        scaled = scaled * column * row
    return coefficients, doubtful


def kernel(
    replicas,
    tensors,
    members,
    tiles,
    *refs,
):
    count = sum(len(chunk) for chunk in members)
    chunks = len(members)
    inputs, outs, rest = refs[:count], refs[count : 2 * count], refs[2 * count :]
    (gathered, flags, raw, laid, half_in, half, quarter_in, quarter,
     stat_pair, stat_cluster, gram_rows, gram_cluster, gathered_v,
     in_sem, half_send, half_recv, pair_send, pair_recv, quarter_send, quarter_recv,
     cluster_send, cluster_recv, row_send, row_recv, gram_row_send, gram_row_recv,
     gram_cluster_send, gram_cluster_recv, out_sem) = rest

    groups = replicas // 4
    replica = lax.axis_index("replica")
    tensor = lax.axis_index("tensor")
    group = replica // 4
    local = replica % 4
    bit = local % 2
    high = local // 2
    pair_size, cluster_size = 2 * tensors, 4 * tensors
    pair_me = bit * tensors + tensor
    cluster_me = local * tensors + tensor

    def pair_device(index):
        return (group * 4 + high * 2 + index // tensors, index % tensors)

    def cluster_device(index):
        return (group * 4 + index // tensors, index % tensors)

    def group_device(index):
        return (index * 4 + local, tensor)

    barrier = pltpu.get_barrier_semaphore()

    def greet(size, me, device):
        def one(step, carry):
            pl.semaphore_signal(
                barrier, inc=1, device_id=device((me + step) % size), device_id_type=MESH
            )
            return carry

        lax.fori_loop(1, size, one, 0)

    greet(cluster_size, cluster_me, cluster_device)
    greet(groups, group, group_device)

    input_copies = []
    number = 0
    for chunk, widths in enumerate(members):
        start = 0
        for width in widths:
            input_copies.append(
                pltpu.make_async_copy(
                    inputs[number].at[0],
                    raw.at[chunk, :, pl.ds(start, width * LANES)],
                    in_sem.at[number],
                )
            )
            start += width * LANES
            number += 1
    for copy in input_copies:
        copy.start()

    rows_of_tile = lax.broadcasted_iota(jnp.int32, (tiles, LANES), 0)
    tile_row = lax.broadcasted_iota(jnp.int32, (8, LANES), 0)

    def spans(chunk):
        start = 0
        for width in members[chunk]:
            yield start, start + width
            start += width

    def bring(chunk):
        first = sum(len(widths) for widths in members[:chunk])
        for number in range(first, first + len(members[chunk])):
            input_copies[number].wait()

        def block(step, carry):
            top = pl.multiple_of(step * 8, 8)
            for column in range(tiles):
                laid[chunk, pl.ds(top * tiles + column, 8, stride=tiles), :] = raw[
                    chunk, pl.ds(top, 8), pl.ds(column * LANES, LANES)
                ]
            return carry

        lax.fori_loop(0, replicas // 8, block, 0)

    def half_copies(chunk):
        view = laid.at[chunk].reshape(groups, 4, tiles, LANES)
        return [
            pltpu.make_async_remote_copy(
                src_ref=view.at[:, 1 - bit + 2 * part],
                dst_ref=half_in.at[chunk, part].reshape(groups, tiles, LANES),
                send_sem=half_send.at[chunk, part],
                recv_sem=half_recv.at[chunk, part],
                device_id=(replica + 1 - 2 * bit, tensor),
                device_id_type=MESH,
            )
            for part in range(2)
        ]

    def quarter_copy(chunk):
        return pltpu.make_async_remote_copy(
            src_ref=half.at[chunk, 1 - high],
            dst_ref=quarter_in.at[chunk],
            send_sem=quarter_send.at[chunk],
            recv_sem=quarter_recv.at[chunk],
            device_id=(replica + 2 - 4 * high, tensor),
            device_id_type=MESH,
        )

    def broadcast(slots, size, me, device, send_sem, recv_sem):
        def one(step, carry):
            pltpu.make_async_remote_copy(
                src_ref=slots.at[me],
                dst_ref=slots.at[me],
                send_sem=send_sem,
                recv_sem=recv_sem,
                device_id=device((me + step) % size),
                device_id_type=MESH,
            ).start()
            return carry

        lax.fori_loop(1, size, one, 0)

    def wait_bytes(ref, semaphore):
        pltpu.make_async_copy(ref, ref, semaphore).wait()

    def tile_at(ref, index, step):
        return ref.at[index + (pl.ds(pl.multiple_of(step * tiles, 8), tiles),)]

    def statistics(chunk, pairs_at, slots, me, mine_is_low):
        def one(step, carry):
            for own, theirs in pairs_at(step):
                carry = (
                    carry[0] + own * theirs,
                    carry[1] + own * own,
                    carry[2] + theirs * theirs,
                )
            return carry

        zero = jnp.zeros((tiles, LANES), jnp.float32)
        cross, own, theirs = lax.fori_loop(0, groups, one, (zero, zero, zero))
        lower = jnp.where(mine_is_low, own, theirs)
        upper = jnp.where(mine_is_low, theirs, own)
        message = jnp.zeros((8, LANES), jnp.float32)
        row = 0
        for start, stop in spans(chunk):
            inside = (rows_of_tile >= start) & (rows_of_tile < stop)
            for value in (cross, lower, upper):
                total = jnp.sum(jnp.where(inside, value, 0.0), axis=0, keepdims=True)
                message = jnp.where(tile_row == row, total, message)
                row += 1
        slots[chunk, me] = message

    def weights(chunk, slots, size, mine_is_low):
        total = slots[chunk, 0]
        for index in range(1, size):
            total = total + slots[chunk, index]
        total = jnp.sum(total, axis=1, keepdims=True)
        own_weight = jnp.zeros((tiles, LANES), jnp.float32)
        their_weight = jnp.zeros((tiles, LANES), jnp.float32)
        for number, (start, stop) in enumerate(spans(chunk)):
            inside = (rows_of_tile >= start) & (rows_of_tile < stop)
            cross = total[3 * number : 3 * number + 1]
            low = lower_weight(cross, total[3 * number + 1 : 3 * number + 2])
            up = lower_weight(cross, total[3 * number + 2 : 3 * number + 3])
            own_weight = jnp.where(inside, jnp.where(mine_is_low, low, up), own_weight)
            their_weight = jnp.where(inside, jnp.where(mine_is_low, up, low), their_weight)
        return own_weight, their_weight

    def half_pair(chunk, part, step):
        own = tile_at(laid, (chunk,), step * 4 + bit + 2 * part)[...]
        return own, tile_at(half_in, (chunk, part), step)[...]

    def quarter_pair(chunk, step):
        own = tile_at(half, (chunk, high), step)[...]
        return own, tile_at(quarter_in, (chunk,), step)[...]

    def send_half(chunk):
        for copy in half_copies(chunk):
            copy.start()

    def half_statistics(chunk):
        for copy in half_copies(chunk):
            copy.wait_recv()
        statistics(
            chunk,
            lambda step: [half_pair(chunk, part, step) for part in range(2)],
            stat_pair,
            pair_me,
            bit == 0,
        )
        broadcast(
            stat_pair.at[chunk], pair_size, pair_me, pair_device, pair_send.at[chunk], pair_recv.at[chunk]
        )

    def half_combine(chunk):
        wait_bytes(stat_pair.at[chunk, pl.ds(0, pair_size - 1)], pair_recv.at[chunk])
        own_weight, their_weight = weights(chunk, stat_pair, pair_size, bit == 0)

        def combine(part):
            def one(step, carry):
                own, theirs = half_pair(chunk, part, step)
                tile_at(half, (chunk, part), step)[...] = own_weight * own + their_weight * theirs
                return carry

            lax.fori_loop(0, groups, one, 0)

        combine(1 - high)
        quarter_copy(chunk).start()
        combine(high)

    def quarter_statistics(chunk):
        quarter_copy(chunk).wait_recv()
        statistics(
            chunk,
            lambda step: [quarter_pair(chunk, step)],
            stat_cluster,
            cluster_me,
            high == 0,
        )
        broadcast(
            stat_cluster.at[chunk],
            cluster_size,
            cluster_me,
            cluster_device,
            cluster_send.at[chunk],
            cluster_recv.at[chunk],
        )

    def quarter_combine(chunk):
        wait_bytes(stat_cluster.at[chunk, pl.ds(0, cluster_size - 1)], cluster_recv.at[chunk])
        own_weight, their_weight = weights(chunk, stat_cluster, cluster_size, high == 0)

        def one(step, carry):
            own, theirs = quarter_pair(chunk, step)
            tile_at(quarter, (chunk,), step)[...] = own_weight * own + their_weight * theirs
            return carry

        lax.fori_loop(0, groups, one, 0)

        def send(step, carry):
            other = (group + step) % groups
            pltpu.make_async_remote_copy(
                src_ref=tile_at(quarter, (chunk,), other),
                dst_ref=tile_at(gathered_v, (chunk,), group),
                send_sem=row_send.at[chunk],
                recv_sem=row_recv.at[chunk],
                device_id=group_device(other),
                device_id_type=MESH,
            ).start()
            return carry

        lax.fori_loop(1, groups, send, 0)
        tile_at(gathered_v, (chunk,), group)[...] = tile_at(quarter, (chunk,), group)[...]

    def side_by_side(chunk, start, stop):
        return jnp.concatenate(
            [
                gathered_v[chunk, pl.ds(column, groups, stride=tiles), :]
                for column in range(start, stop)
            ],
            axis=1,
        )

    def gram_first(chunk):
        wait_bytes(gathered_v.at[chunk, pl.ds(0, (groups - 1) * tiles)], row_recv.at[chunk])
        pltpu.make_async_copy(gathered_v.at[chunk], gathered.at[chunk], out_sem.at[chunk]).start()
        grams = []
        for start, stop in spans(chunk):
            vectors = side_by_side(chunk, start, stop)
            grams.append(
                lax.dot_general(
                    vectors,
                    vectors,
                    (((1,), (1,)), ((), ())),
                    precision=lax.Precision.HIGHEST,
                    preferred_element_type=jnp.float32,
                )
            )
        grams.append(jnp.zeros((groups, LANES - groups * len(grams)), jnp.float32))
        gram_rows[chunk, group] = jnp.concatenate(grams, axis=1)
        broadcast(
            gram_rows.at[chunk], groups, group, group_device, gram_row_send.at[chunk], gram_row_recv.at[chunk]
        )

    def gram_second(chunk):
        wait_bytes(gram_rows.at[chunk, pl.ds(0, groups - 1)], gram_row_recv.at[chunk])
        total = gram_rows[chunk, 0]
        for index in range(1, groups):
            total = total + gram_rows[chunk, index]
        gram_cluster[chunk, cluster_me] = total
        broadcast(
            gram_cluster.at[chunk],
            cluster_size,
            cluster_me,
            cluster_device,
            gram_cluster_send.at[chunk],
            gram_cluster_recv.at[chunk],
        )

    def finish(chunk):
        wait_bytes(gram_cluster.at[chunk, pl.ds(0, cluster_size - 1)], gram_cluster_recv.at[chunk])
        total = gram_cluster[chunk, 0]
        for index in range(1, cluster_size):
            total = total + gram_cluster[chunk, index]
        first = sum(len(widths) for widths in members[:chunk])
        worst = jnp.zeros((1, 1), jnp.float32)
        for number, (start, stop) in enumerate(spans(chunk)):
            coefficients, doubtful = tree_weights(total[:, groups * number : groups * (number + 1)])
            vectors = side_by_side(chunk, start, stop)
            outs[first + number][...] = jnp.sum(coefficients * vectors, axis=0, keepdims=True)
            worst = jnp.maximum(worst, jnp.max(doubtful, axis=0, keepdims=True))
        flags[chunk] = jnp.broadcast_to(worst, (8, LANES))

    bring(0)
    pl.semaphore_wait(barrier, cluster_size + groups - 2)
    send_half(0)
    for chunk in range(1, chunks):
        bring(chunk)
        send_half(chunk)
    stages = [
        half_statistics,
        half_combine,
        quarter_statistics,
        quarter_combine,
        gram_first,
        gram_second,
        finish,
    ]
    order = sorted(
        (chunk * 2 + stage, chunk, stage) for chunk in range(chunks) for stage in range(len(stages))
    )
    for _, chunk, stage in order:
        stages[stage](chunk)

    for chunk in range(chunks):
        for copy in half_copies(chunk):
            copy.wait_send()
        quarter_copy(chunk).wait_send()
        wait_bytes(stat_pair.at[chunk, pl.ds(0, pair_size - 1)], pair_send.at[chunk])
        wait_bytes(stat_cluster.at[chunk, pl.ds(0, cluster_size - 1)], cluster_send.at[chunk])
        wait_bytes(gathered_v.at[chunk, pl.ds(0, (groups - 1) * tiles)], row_send.at[chunk])
        wait_bytes(gram_rows.at[chunk, pl.ds(0, groups - 1)], gram_row_send.at[chunk])
        wait_bytes(gram_cluster.at[chunk, pl.ds(0, cluster_size - 1)], gram_cluster_send.at[chunk])
        pltpu.make_async_copy(gathered_v.at[chunk], gathered.at[chunk], out_sem.at[chunk]).wait()


def level_by_level(vectors):
    while vectors.shape[0] > 1:
        lower, upper = vectors[0::2], vectors[1::2]
        totals = lax.psum(
            jnp.stack(
                [
                    jnp.sum(lower * upper, axis=(1, 2)),
                    jnp.sum(lower * lower, axis=(1, 2)),
                    jnp.sum(upper * upper, axis=(1, 2)),
                ]
            ),
            ("replica", "tensor"),
        )
        low = lower_weight(totals[0], totals[1])[:, None, None]
        up = lower_weight(totals[0], totals[2])[:, None, None]
        vectors = low * lower + up * upper
    return vectors.reshape(1, -1)


def per_device(*grads):
    replicas, tensors = lax.axis_size("replica"), lax.axis_size("tensor")
    groups = replicas // 4
    widths = [member.shape[2] // LANES for member in grads]
    tiles = max(widths)
    members = []
    for width in widths:
        if members and sum(members[-1]) + width <= tiles:
            members[-1].append(width)
        else:
            members.append([width])
    chunks = len(members)
    f32 = jnp.float32
    dma = pltpu.SemaphoreType.DMA
    results = pl.pallas_call(
        functools.partial(kernel, replicas, tensors, members, tiles),
        out_shape=[jax.ShapeDtypeStruct((1, member.shape[2]), f32) for member in grads]
        + [
            jax.ShapeDtypeStruct((chunks, groups * tiles, LANES), f32),
            jax.ShapeDtypeStruct((chunks, 8, LANES), f32),
        ],
        in_specs=[pl.BlockSpec(memory_space=pl.ANY)] * len(grads),
        out_specs=[pl.BlockSpec(memory_space=pltpu.VMEM)] * len(grads)
        + [pl.BlockSpec(memory_space=pl.ANY), pl.BlockSpec(memory_space=pltpu.VMEM)],
        scratch_shapes=[
            pltpu.VMEM((chunks, replicas, tiles * LANES), f32),
            pltpu.VMEM((chunks, replicas * tiles, LANES), f32),
            pltpu.VMEM((chunks, 2, groups * tiles, LANES), f32),
            pltpu.VMEM((chunks, 2, groups * tiles, LANES), f32),
            pltpu.VMEM((chunks, groups * tiles, LANES), f32),
            pltpu.VMEM((chunks, groups * tiles, LANES), f32),
            pltpu.VMEM((chunks, 2 * tensors, 8, LANES), f32),
            pltpu.VMEM((chunks, 4 * tensors, 8, LANES), f32),
            pltpu.VMEM((chunks, groups, groups, LANES), f32),
            pltpu.VMEM((chunks, 4 * tensors, groups, LANES), f32),
            pltpu.VMEM((chunks, groups * tiles, LANES), f32),
            dma((len(grads),)),
            dma((chunks, 2)),
            dma((chunks, 2)),
        ]
        + [dma((chunks,))] * 13,
        compiler_params=pltpu.CompilerParams(
            collective_id=0, has_side_effects=True, vmem_limit_bytes=40 * 1024 * 1024
        ),
    )(*grads)
    combined, gathered, flags = results[: len(grads)], results[len(grads)], results[-1]

    def again(combined, gathered):
        outputs = []
        for chunk, in_chunk in enumerate(members):
            vectors = gathered[chunk].reshape(groups, tiles, LANES)
            start = 0
            for width in in_chunk:
                outputs.append(level_by_level(vectors[:, start : start + width]))
                start += width
        return outputs

    return tuple(
        lax.cond(
            jnp.max(flags) > 0.0,
            again,
            lambda combined, gathered: list(combined),
            list(combined),
            gathered,
        )
    )


def solution(mesh):
    return jax.shard_map(
        per_device,
        mesh=mesh,
        in_specs=(P("replica", None, "tensor"),) * 4,
        out_specs=(P("replica", "tensor"),) * 4,
        check_vma=False,
    )
```

```python
import functools

import jax
import jax.numpy as jnp
from jax import lax
from jax.experimental import pallas as pl
from jax.experimental.pallas import tpu as pltpu
from jax.sharding import PartitionSpec as P

EPSILON = 1e-06
LANES = 128
TRUSTED = 0.03
MESH = pl.DeviceIdType.MESH
ORDER = (
    "s0A s1A b0B s0B b0C r0A t0A s1B c0A s0C r0B t0B s1C c0B r1A t1A r0C t0C c1A c0C r1B t1B c1B "
    "r2A t2A r1C t1C c1C u2A r2B t2B u2B r2C t2C u2C f2A f2B f2C"
)


def lower_weight(cross, norm):
    return 1.0 - cross / (2.0 * (norm + EPSILON))


def tree_weights(gram):
    count = gram.shape[0]
    across = lax.broadcasted_iota(jnp.int32, (count, count), 1)
    down = lax.broadcasted_iota(jnp.int32, (count, count), 0)
    coefficients = jnp.ones((count, 1), jnp.float32)
    doubtful = jnp.zeros((count, 1), jnp.float32)
    scaled = gram
    for level in range(count.bit_length() - 1):
        same = (across >> level) == (down >> level)
        either = (across >> (level + 1)) == (down >> (level + 1))
        own = jnp.where(same, scaled, 0.0)
        sibling = jnp.where(either, scaled, 0.0) - own
        sizes = jnp.abs(own)

        def column_of(terms):
            partial = jnp.sum(terms, axis=0, keepdims=True)
            return jnp.sum(jnp.where(same, partial, 0.0), axis=1, keepdims=True)

        def row_of(terms):
            partial = jnp.sum(terms, axis=1, keepdims=True)
            return jnp.sum(jnp.where(same, partial, 0.0), axis=0, keepdims=True)

        norm = column_of(own)
        column = lower_weight(column_of(sibling), norm)
        row = lower_weight(row_of(sibling), row_of(own))
        doubtful = jnp.maximum(
            doubtful, jnp.where(norm < TRUSTED * column_of(sizes), 1.0, 0.0)
        )
        coefficients = coefficients * column
        scaled = scaled * column * row
    return coefficients, doubtful


def kernel(
    replicas,
    tensors,
    members,
    tiles,
    *refs,
):
    count = sum(len(chunk) for chunk in members)
    chunks = len(members)
    inputs, outs, rest = refs[:count], refs[count : 2 * count], refs[2 * count :]
    (gathered, flag, raw, laid, half_in, half, quarter_in, quarter, gathered_v, doubts,
     half_shares, half_totals, quarter_shares, quarter_totals, gram_shares, gram_parts, gram_totals,
     in_sem, half_send, half_recv, *semaphores) = rest
    (quarter_send, quarter_recv, row_send, row_recv, out_sem,
     half_share_send, half_share_recv, half_total_send, half_total_recv,
     quarter_share_send, quarter_share_recv, quarter_total_send, quarter_total_recv,
     gram_share_send, gram_share_recv, gram_part_send, gram_part_recv,
     gram_total_send, gram_total_recv) = semaphores

    groups = replicas // 4
    replica = lax.axis_index("replica")
    tensor = lax.axis_index("tensor")
    group = replica // 4
    local = replica % 4
    bit = local % 2
    high = local // 2

    def tensor_device(index):
        return (replica, index)

    def pair_device(index):
        return (group * 4 + high * 2 + index, tensor)

    def local_device(index):
        return (group * 4 + index, tensor)

    def group_device(index):
        return (index * 4 + local, tensor)

    barrier = pltpu.get_barrier_semaphore()

    def greet(size, me, device):
        def one(step, carry):
            pl.semaphore_signal(
                barrier, inc=1, device_id=device((me + step) % size), device_id_type=MESH
            )
            return carry

        lax.fori_loop(1, size, one, 0)

    greet(tensors, tensor, tensor_device)
    greet(4, local, local_device)
    greet(groups, group, group_device)

    input_copies = []
    number = 0
    for chunk, widths in enumerate(members):
        start = 0
        for width in widths:
            input_copies.append(
                pltpu.make_async_copy(
                    inputs[number].at[0],
                    raw.at[chunk, :, pl.ds(start, width * LANES)],
                    in_sem.at[number],
                )
            )
            start += width * LANES
            number += 1
    for copy in input_copies:
        copy.start()

    rows_of_tile = lax.broadcasted_iota(jnp.int32, (tiles, LANES), 0)
    tile_row = lax.broadcasted_iota(jnp.int32, (8, LANES), 0)

    def spans(chunk):
        start = 0
        for width in members[chunk]:
            yield start, start + width
            start += width

    def bring(chunk):
        first = sum(len(widths) for widths in members[:chunk])
        for number in range(first, first + len(members[chunk])):
            input_copies[number].wait()

        def block(step, carry):
            top = pl.multiple_of(step * 8, 8)
            for column in range(tiles):
                laid[chunk, pl.ds(top * tiles + column, 8, stride=tiles), :] = raw[
                    chunk, pl.ds(top, 8), pl.ds(column * LANES, LANES)
                ]
            return carry

        lax.fori_loop(0, replicas // 8, block, 0)

    def half_copy(part, chunk):
        return pltpu.make_async_remote_copy(
            src_ref=laid.at[chunk].reshape(groups, 4, tiles, LANES).at[:, 1 - bit + 2 * part],
            dst_ref=half_in.at[chunk, part].reshape(groups, tiles, LANES),
            send_sem=half_send.at[chunk, part],
            recv_sem=half_recv.at[chunk, part],
            device_id=(replica + 1 - 2 * bit, tensor),
            device_id_type=MESH,
        )

    def quarter_copy(chunk):
        return pltpu.make_async_remote_copy(
            src_ref=half.at[chunk, 1 - high],
            dst_ref=quarter_in.at[chunk],
            send_sem=quarter_send.at[chunk],
            recv_sem=quarter_recv.at[chunk],
            device_id=(replica + 2 - 4 * high, tensor),
            device_id_type=MESH,
        )

    def broadcast(chunk, slots, size, me, device, send_sem, recv_sem):
        def one(step, carry):
            pltpu.make_async_remote_copy(
                src_ref=slots.at[chunk, me],
                dst_ref=slots.at[chunk, me],
                send_sem=send_sem.at[chunk],
                recv_sem=recv_sem.at[chunk],
                device_id=device((me + step) % size),
                device_id_type=MESH,
            ).start()
            return carry

        lax.fori_loop(1, size, one, 0)

    def wait_bytes(ref, semaphore):
        pltpu.make_async_copy(ref, ref, semaphore).wait()

    def collect(chunk, slots, size, recv_sem):
        wait_bytes(slots.at[chunk, pl.ds(0, size - 1)], recv_sem.at[chunk])
        total = slots[chunk, 0]
        for index in range(1, size):
            total = total + slots[chunk, index]
        return total

    def tile_at(ref, index, step):
        return ref.at[index + (pl.ds(pl.multiple_of(step * tiles, 8), tiles),)]

    def statistics(chunk, pairs_at, mine_is_low):
        def one(step, carry):
            for own, theirs in pairs_at(step):
                carry = (
                    carry[0] + own * theirs,
                    carry[1] + own * own,
                    carry[2] + theirs * theirs,
                )
            return carry

        zero = jnp.zeros((tiles, LANES), jnp.float32)
        cross, own, theirs = lax.fori_loop(0, groups, one, (zero, zero, zero))
        lower = jnp.where(mine_is_low, own, theirs)
        upper = jnp.where(mine_is_low, theirs, own)
        message = jnp.zeros((8, LANES), jnp.float32)
        row = 0
        for start, stop in spans(chunk):
            inside = (rows_of_tile >= start) & (rows_of_tile < stop)
            for value in (cross, lower, upper):
                total = jnp.sum(jnp.where(inside, value, 0.0), axis=0, keepdims=True)
                message = jnp.where(tile_row == row, total, message)
                row += 1
        return message

    def weights(chunk, total, mine_is_low):
        total = jnp.sum(total, axis=1, keepdims=True)
        own_weight = jnp.zeros((tiles, LANES), jnp.float32)
        their_weight = jnp.zeros((tiles, LANES), jnp.float32)
        for number, (start, stop) in enumerate(spans(chunk)):
            inside = (rows_of_tile >= start) & (rows_of_tile < stop)
            cross = total[3 * number : 3 * number + 1]
            low = lower_weight(cross, total[3 * number + 1 : 3 * number + 2])
            up = lower_weight(cross, total[3 * number + 2 : 3 * number + 3])
            own_weight = jnp.where(inside, jnp.where(mine_is_low, low, up), own_weight)
            their_weight = jnp.where(inside, jnp.where(mine_is_low, up, low), their_weight)
        return own_weight, their_weight

    def half_pair(chunk, part, step):
        own = tile_at(laid, (chunk,), step * 4 + bit + 2 * part)[...]
        return own, tile_at(half_in, (chunk, part), step)[...]

    def quarter_pair(chunk, step):
        own = tile_at(half, (chunk, high), step)[...]
        return own, tile_at(quarter_in, (chunk,), step)[...]

    def send_half(part, chunk):
        half_copy(part, chunk).start()

    def half_share(chunk):
        for part in range(2):
            half_copy(part, chunk).wait_recv()
        half_shares[chunk, tensor] = statistics(
            chunk, lambda step: [half_pair(chunk, part, step) for part in range(2)], bit == 0
        )
        broadcast(chunk, half_shares, tensors, tensor, tensor_device, half_share_send, half_share_recv)

    def half_total(chunk):
        half_totals[chunk, bit] = collect(chunk, half_shares, tensors, half_share_recv)
        broadcast(chunk, half_totals, 2, bit, pair_device, half_total_send, half_total_recv)

    def half_combine(chunk):
        total = collect(chunk, half_totals, 2, half_total_recv)
        own_weight, their_weight = weights(chunk, total, bit == 0)

        def combine(part):
            def one(step, carry):
                own, theirs = half_pair(chunk, part, step)
                tile_at(half, (chunk, part), step)[...] = own_weight * own + their_weight * theirs
                return carry

            lax.fori_loop(0, groups, one, 0)

        combine(1 - high)
        quarter_copy(chunk).start()
        combine(high)

    def quarter_share(chunk):
        quarter_copy(chunk).wait_recv()
        quarter_shares[chunk, tensor] = statistics(
            chunk, lambda step: [quarter_pair(chunk, step)], high == 0
        )
        broadcast(
            chunk, quarter_shares, tensors, tensor, tensor_device, quarter_share_send, quarter_share_recv
        )

    def quarter_total(chunk):
        quarter_totals[chunk, local] = collect(chunk, quarter_shares, tensors, quarter_share_recv)
        broadcast(chunk, quarter_totals, 4, local, local_device, quarter_total_send, quarter_total_recv)

    def quarter_combine(chunk):
        total = collect(chunk, quarter_totals, 4, quarter_total_recv)
        own_weight, their_weight = weights(chunk, total, high == 0)

        def one(step, carry):
            own, theirs = quarter_pair(chunk, step)
            tile_at(quarter, (chunk,), step)[...] = own_weight * own + their_weight * theirs
            return carry

        lax.fori_loop(0, groups, one, 0)

        def send(step, carry):
            other = (group + step) % groups
            pltpu.make_async_remote_copy(
                src_ref=tile_at(quarter, (chunk,), other),
                dst_ref=tile_at(gathered_v, (chunk,), group),
                send_sem=row_send.at[chunk],
                recv_sem=row_recv.at[chunk],
                device_id=group_device(other),
                device_id_type=MESH,
            ).start()
            return carry

        lax.fori_loop(1, groups, send, 0)
        tile_at(gathered_v, (chunk,), group)[...] = tile_at(quarter, (chunk,), group)[...]

    def side_by_side(chunk, start, stop):
        return jnp.concatenate(
            [
                gathered_v[chunk, pl.ds(column, groups, stride=tiles), :]
                for column in range(start, stop)
            ],
            axis=1,
        )

    def gram_share(chunk):
        wait_bytes(gathered_v.at[chunk, pl.ds(0, (groups - 1) * tiles)], row_recv.at[chunk])
        pltpu.make_async_copy(gathered_v.at[chunk], gathered.at[chunk], out_sem.at[chunk]).start()
        pieces = []
        for start, stop in spans(chunk):
            vectors = side_by_side(chunk, start, stop)
            gram = lax.dot_general(
                vectors,
                vectors,
                (((1,), (1,)), ((), ())),
                precision=lax.Precision.HIGHEST,
                preferred_element_type=jnp.float32,
            )
            pieces += [gram[top : top + 8] for top in range(0, groups, 8)]
        pieces.append(jnp.zeros((8, LANES - groups * len(pieces)), jnp.float32))
        gram_shares[chunk, tensor] = jnp.concatenate(pieces, axis=1)
        broadcast(chunk, gram_shares, tensors, tensor, tensor_device, gram_share_send, gram_share_recv)

    def gram_part(chunk):
        gram_parts[chunk, local] = collect(chunk, gram_shares, tensors, gram_share_recv)
        broadcast(chunk, gram_parts, 4, local, local_device, gram_part_send, gram_part_recv)

    def gram_total(chunk):
        gram_totals[chunk, group] = collect(chunk, gram_parts, 4, gram_part_recv)
        broadcast(chunk, gram_totals, groups, group, group_device, gram_total_send, gram_total_recv)

    def finish(chunk):
        total = collect(chunk, gram_totals, groups, gram_total_recv)
        first = sum(len(widths) for widths in members[:chunk])
        worst = jnp.zeros((1, 1), jnp.float32)
        blocks = groups // 8
        for number, (start, stop) in enumerate(spans(chunk)):
            gram = jnp.concatenate(
                [
                    total[:, groups * block : groups * (block + 1)]
                    for block in range(number * blocks, (number + 1) * blocks)
                ],
                axis=0,
            )
            coefficients, doubtful = tree_weights(gram)
            vectors = side_by_side(chunk, start, stop)
            outs[first + number][...] = jnp.sum(coefficients * vectors, axis=0, keepdims=True)
            worst = jnp.maximum(worst, jnp.max(doubtful, axis=0, keepdims=True))
        doubts[chunk] = jnp.broadcast_to(worst, (8, LANES))

    bring(0)
    pl.semaphore_wait(barrier, tensors + 4 + groups - 3)
    steps = {
        "s0": functools.partial(send_half, 0),
        "s1": functools.partial(send_half, 1),
        "b0": bring,
        "r0": half_share,
        "t0": half_total,
        "c0": half_combine,
        "r1": quarter_share,
        "t1": quarter_total,
        "c1": quarter_combine,
        "r2": gram_share,
        "t2": gram_part,
        "u2": gram_total,
        "f2": finish,
    }
    for step in ORDER.split():
        steps[step[:2]]("ABC".index(step[2]))

    worst = doubts[0]
    for chunk in range(1, chunks):
        worst = jnp.maximum(worst, doubts[chunk])
    flag[0] = jnp.max(worst)

    for chunk in range(chunks):
        for part in range(2):
            half_copy(part, chunk).wait_send()
        quarter_copy(chunk).wait_send()
        wait_bytes(gathered_v.at[chunk, pl.ds(0, (groups - 1) * tiles)], row_send.at[chunk])
        for slots, size, sent in (
            (half_shares, tensors, half_share_send),
            (half_totals, 2, half_total_send),
            (quarter_shares, tensors, quarter_share_send),
            (quarter_totals, 4, quarter_total_send),
            (gram_shares, tensors, gram_share_send),
            (gram_parts, 4, gram_part_send),
            (gram_totals, groups, gram_total_send),
        ):
            wait_bytes(slots.at[chunk, pl.ds(0, size - 1)], sent.at[chunk])
        pltpu.make_async_copy(gathered_v.at[chunk], gathered.at[chunk], out_sem.at[chunk]).wait()


def level_by_level(vectors):
    while vectors.shape[0] > 1:
        lower, upper = vectors[0::2], vectors[1::2]
        totals = lax.psum(
            jnp.stack(
                [
                    jnp.sum(lower * upper, axis=(1, 2)),
                    jnp.sum(lower * lower, axis=(1, 2)),
                    jnp.sum(upper * upper, axis=(1, 2)),
                ]
            ),
            ("replica", "tensor"),
        )
        low = lower_weight(totals[0], totals[1])[:, None, None]
        up = lower_weight(totals[0], totals[2])[:, None, None]
        vectors = low * lower + up * upper
    return vectors.reshape(1, -1)


def per_device(*grads):
    replicas, tensors = lax.axis_size("replica"), lax.axis_size("tensor")
    groups = replicas // 4
    widths = [member.shape[2] // LANES for member in grads]
    tiles = max(widths)
    members = []
    for width in widths:
        if members and sum(members[-1]) + width <= tiles:
            members[-1].append(width)
        else:
            members.append([width])
    chunks = len(members)
    f32 = jnp.float32
    dma = pltpu.SemaphoreType.DMA
    results = pl.pallas_call(
        functools.partial(kernel, replicas, tensors, members, tiles),
        out_shape=[jax.ShapeDtypeStruct((1, member.shape[2]), f32) for member in grads]
        + [
            jax.ShapeDtypeStruct((chunks, groups * tiles, LANES), f32),
            jax.ShapeDtypeStruct((1,), f32),
        ],
        in_specs=[pl.BlockSpec(memory_space=pl.ANY)] * len(grads),
        out_specs=[pl.BlockSpec(memory_space=pltpu.VMEM)] * len(grads)
        + [pl.BlockSpec(memory_space=pl.ANY), pl.BlockSpec(memory_space=pltpu.SMEM)],
        scratch_shapes=[
            pltpu.VMEM((chunks, replicas, tiles * LANES), f32),
            pltpu.VMEM((chunks, replicas * tiles, LANES), f32),
            pltpu.VMEM((chunks, 2, groups * tiles, LANES), f32),
            pltpu.VMEM((chunks, 2, groups * tiles, LANES), f32),
            pltpu.VMEM((chunks, groups * tiles, LANES), f32),
            pltpu.VMEM((chunks, groups * tiles, LANES), f32),
            pltpu.VMEM((chunks, groups * tiles, LANES), f32),
            pltpu.VMEM((chunks, 8, LANES), f32),
        ]
        + [
            pltpu.VMEM((chunks, size, 8, LANES), f32)
            for size in (tensors, 2, tensors, 4, tensors, 4, groups)
        ]
        + [
            dma((len(grads),)),
            dma((chunks, 2)),
            dma((chunks, 2)),
        ]
        + [dma((chunks,))] * 19,
        compiler_params=pltpu.CompilerParams(
            collective_id=0, has_side_effects=True, vmem_limit_bytes=60 * 1024 * 1024
        ),
    )(*grads)
    combined, gathered, flag = results[: len(grads)], results[len(grads)], results[-1]

    def again(combined, gathered):
        outputs = []
        for chunk, in_chunk in enumerate(members):
            vectors = gathered[chunk].reshape(groups, tiles, LANES)
            start = 0
            for width in in_chunk:
                outputs.append(level_by_level(vectors[:, start : start + width]))
                start += width
        return outputs

    return tuple(
        lax.cond(
            flag[0] > 0.0,
            again,
            lambda combined, gathered: list(combined),
            list(combined),
            gathered,
        )
    )


def solution(mesh):
    return jax.shard_map(
        per_device,
        mesh=mesh,
        in_specs=(P("replica", None, "tensor"),) * 4,
        out_specs=(P("replica", "tensor"),) * 4,
        check_vma=False,
    )
```

```python
import functools

import jax
import jax.numpy as jnp
from jax import lax
from jax.experimental import pallas as pl
from jax.experimental.pallas import tpu as pltpu
from jax.sharding import PartitionSpec as P

EPSILON = 1e-06
LANES = 128
TRUSTED = 0.03
MESH = pl.DeviceIdType.MESH
ORDER = (
    "s0A", "s1A", "b0B", "s0B", "b0C", "r0A", "s1B", "c0A", "q1A", "r0B", "s0C", "s1C", "r1A",
    "c0B", "q1B", "r0C", "c1A", "r1B", "c0C", "w1A", "q1C", "c1B", "r1C", "w1B", "c1C", "w1C",
    "r2A", "r2B", "r2C", "g2C", "u2C", "f2C",
)


def lower_weight(cross, norm):
    return 1.0 - cross / (2.0 * (norm + EPSILON))


def tree_weights(gram):
    count = gram.shape[0]
    across = lax.broadcasted_iota(jnp.int32, (count, count), 1)
    down = lax.broadcasted_iota(jnp.int32, (count, count), 0)
    coefficients = jnp.ones((count, 1), jnp.float32)
    doubtful = jnp.zeros((count, 1), jnp.float32)
    scaled = gram
    for level in range(count.bit_length() - 1):
        same = (across >> level) == (down >> level)
        either = (across >> (level + 1)) == (down >> (level + 1))
        own = jnp.where(same, scaled, 0.0)
        sibling = jnp.where(either, scaled, 0.0) - own
        sizes = jnp.abs(own)

        def column_of(terms):
            partial = jnp.sum(terms, axis=0, keepdims=True)
            return jnp.sum(jnp.where(same, partial, 0.0), axis=1, keepdims=True)

        def row_of(terms):
            partial = jnp.sum(terms, axis=1, keepdims=True)
            return jnp.sum(jnp.where(same, partial, 0.0), axis=0, keepdims=True)

        norm = column_of(own)
        column = lower_weight(column_of(sibling), norm)
        row = lower_weight(row_of(sibling), row_of(own))
        doubtful = jnp.maximum(
            doubtful, jnp.where(norm < TRUSTED * column_of(sizes), 1.0, 0.0)
        )
        coefficients = coefficients * column
        scaled = scaled * column * row
    return coefficients, doubtful


def kernel(
    replicas,
    tensors,
    members,
    tiles,
    *refs,
):
    count = sum(len(chunk) for chunk in members)
    chunks = len(members)
    inputs, outs, rest = refs[:count], refs[count : 2 * count], refs[2 * count :]
    (gathered, flag, raw, laid, half_in, half, quarter_in, quarter, gathered_v, grams,
     half_sums, quarter_sums, gram_parts, gram_totals,
     in_sem, half_send, half_recv, *semaphores) = rest
    (quarter_send, quarter_recv, row_send, row_recv, out_sem,
     half_sum_send, half_sum_recv, quarter_sum_send, quarter_sum_recv,
     gram_part_send, gram_part_recv, gram_total_send, gram_total_recv) = semaphores

    groups = replicas // 4
    replica = lax.axis_index("replica")
    tensor = lax.axis_index("tensor")
    group = replica // 4
    local = replica % 4
    bit = local % 2
    high = local // 2

    pair_me, cluster_me = bit * tensors + tensor, local * tensors + tensor
    pair_size, cluster_size = 2 * tensors, 4 * tensors

    def pair_device(index):
        return (group * 4 + high * 2 + index // tensors, index % tensors)

    def cluster_device(index):
        return (group * 4 + index // tensors, index % tensors)

    def group_device(index):
        return (index * 4 + local, tensor)

    barrier = pltpu.get_barrier_semaphore()

    def greet(size, me, device):
        def one(step, carry):
            pl.semaphore_signal(
                barrier, inc=1, device_id=device((me + step) % size), device_id_type=MESH
            )
            return carry

        lax.fori_loop(1, size, one, 0)

    greet(cluster_size, cluster_me, cluster_device)
    greet(groups, group, group_device)

    input_copies = []
    number = 0
    for chunk, widths in enumerate(members):
        start = 0
        for width in widths:
            input_copies.append(
                pltpu.make_async_copy(
                    inputs[number].at[0],
                    raw.at[chunk, :, pl.ds(start, width * LANES)],
                    in_sem.at[number],
                )
            )
            start += width * LANES
            number += 1
    for copy in input_copies:
        copy.start()

    rows_of_tile = lax.broadcasted_iota(jnp.int32, (tiles, LANES), 0)
    lane = lax.broadcasted_iota(jnp.int32, (1, LANES), 1)

    def spans(chunk):
        start = 0
        for width in members[chunk]:
            yield start, start + width
            start += width

    def bring(chunk):
        first = sum(len(widths) for widths in members[:chunk])
        for number in range(first, first + len(members[chunk])):
            input_copies[number].wait()

        def block(step, carry):
            top = pl.multiple_of(step * 8, 8)
            for column in range(tiles):
                laid[chunk, pl.ds(top * tiles + column, 8, stride=tiles), :] = raw[
                    chunk, pl.ds(top, 8), pl.ds(column * LANES, LANES)
                ]
            return carry

        lax.fori_loop(0, replicas // 8, block, 0)

    def half_copy(part, chunk):
        return pltpu.make_async_remote_copy(
            src_ref=laid.at[chunk].reshape(groups, 4, tiles, LANES).at[:, 1 - bit + 2 * part],
            dst_ref=half_in.at[chunk, part].reshape(groups, tiles, LANES),
            send_sem=half_send.at[chunk, part],
            recv_sem=half_recv.at[chunk, part],
            device_id=(replica + 1 - 2 * bit, tensor),
            device_id_type=MESH,
        )

    def quarter_copy(part, chunk):
        rows = pl.ds(part * (groups // 2) * tiles, groups // 2 * tiles)
        return pltpu.make_async_remote_copy(
            src_ref=half.at[chunk, 1 - high, rows],
            dst_ref=quarter_in.at[chunk, rows],
            send_sem=quarter_send.at[chunk, part],
            recv_sem=quarter_recv.at[chunk, part],
            device_id=(replica + 2 - 4 * high, tensor),
            device_id_type=MESH,
        )

    def broadcast(chunk, slots, size, me, device, send_sem, recv_sem):
        def one(step, carry):
            pltpu.make_async_remote_copy(
                src_ref=slots.at[chunk, me],
                dst_ref=slots.at[chunk, me],
                send_sem=send_sem.at[chunk],
                recv_sem=recv_sem.at[chunk],
                device_id=device((me + step) % size),
                device_id_type=MESH,
            ).start()
            return carry

        lax.fori_loop(1, size, one, 0)

    def wait_bytes(ref, semaphore):
        pltpu.make_async_copy(ref, ref, semaphore).wait()

    def collect(chunk, slots, size, recv_sem):
        wait_bytes(slots.at[chunk, pl.ds(0, size - 1)], recv_sem.at[chunk])
        total = slots[chunk, 0]
        for index in range(1, size):
            total = total + slots[chunk, index]
        return total

    def tile_at(ref, index, step):
        return ref.at[index + (pl.ds(pl.multiple_of(step * tiles, 8), tiles),)]

    def statistics(chunk, pairs_at, mine_is_low):
        def one(step, carry):
            for own, theirs in pairs_at(step):
                carry = (
                    carry[0] + own * theirs,
                    carry[1] + own * own,
                    carry[2] + theirs * theirs,
                )
            return carry

        zero = jnp.zeros((tiles, LANES), jnp.float32)
        cross, own, theirs = lax.fori_loop(0, groups, one, (zero, zero, zero))
        lower = jnp.where(mine_is_low, own, theirs)
        upper = jnp.where(mine_is_low, theirs, own)
        message = jnp.zeros((1, LANES), jnp.float32)
        place = 0
        for start, stop in spans(chunk):
            inside = (rows_of_tile >= start) & (rows_of_tile < stop)
            for value in (cross, lower, upper):
                total = jnp.sum(jnp.where(inside, value, 0.0), axis=0, keepdims=True)
                total = jnp.sum(total, axis=1, keepdims=True)
                message = jnp.where(lane == place, total, message)
                place += 1
        return message

    def weights(chunk, total, mine_is_low):
        own_weight = jnp.zeros((tiles, LANES), jnp.float32)
        their_weight = jnp.zeros((tiles, LANES), jnp.float32)
        for number, (start, stop) in enumerate(spans(chunk)):
            inside = (rows_of_tile >= start) & (rows_of_tile < stop)
            cross, low_norm, up_norm = (
                total[:, 3 * number + place : 3 * number + place + 1] for place in range(3)
            )
            low = lower_weight(cross, low_norm)
            up = lower_weight(cross, up_norm)
            own_weight = jnp.where(inside, jnp.where(mine_is_low, low, up), own_weight)
            their_weight = jnp.where(inside, jnp.where(mine_is_low, up, low), their_weight)
        return own_weight, their_weight

    def half_pair(chunk, part, step):
        own = tile_at(laid, (chunk,), step * 4 + bit + 2 * part)[...]
        return own, tile_at(half_in, (chunk, part), step)[...]

    def quarter_pair(chunk, step):
        own = tile_at(half, (chunk, high), step)[...]
        return own, tile_at(quarter_in, (chunk,), step)[...]

    kept, others = {}, {}

    def send_half(part, chunk):
        half_copy(part, chunk).start()

    def half_sum(chunk):
        for part in range(2):
            half_copy(part, chunk).wait_recv()
        half_sums[chunk, pair_me] = statistics(
            chunk, lambda step: [half_pair(chunk, part, step) for part in range(2)], bit == 0
        )
        broadcast(chunk, half_sums, pair_size, pair_me, pair_device, half_sum_send, half_sum_recv)

    def half_combine(chunk):
        total = collect(chunk, half_sums, pair_size, half_sum_recv)
        own_weight, their_weight = weights(chunk, total, bit == 0)

        def combine(part, start, stop):
            def one(step, carry):
                own, theirs = half_pair(chunk, part, step)
                tile_at(half, (chunk, part), step)[...] = own_weight * own + their_weight * theirs
                return carry

            lax.fori_loop(start, stop, one, 0)

        combine(1 - high, 0, groups // 2)
        quarter_copy(0, chunk).start()
        combine(1 - high, groups // 2, groups)
        kept[chunk] = lambda: combine(high, 0, groups)

    def send_quarter(chunk):
        quarter_copy(1, chunk).start()
        kept[chunk]()

    def quarter_sum(chunk):
        for part in range(2):
            quarter_copy(part, chunk).wait_recv()
        quarter_sums[chunk, cluster_me] = statistics(
            chunk, lambda step: [quarter_pair(chunk, step)], high == 0
        )
        broadcast(
            chunk, quarter_sums, cluster_size, cluster_me, cluster_device, quarter_sum_send, quarter_sum_recv
        )

    def quarter_combine(chunk):
        total = collect(chunk, quarter_sums, cluster_size, quarter_sum_recv)
        own_weight, their_weight = weights(chunk, total, high == 0)

        def combined(index):
            own, theirs = quarter_pair(chunk, index)
            return own_weight * own + their_weight * theirs

        def send(step, carry):
            other = (group + step) % groups
            tile_at(quarter, (chunk,), other)[...] = combined(other)
            pltpu.make_async_remote_copy(
                src_ref=tile_at(quarter, (chunk,), other),
                dst_ref=tile_at(gathered_v, (chunk,), group),
                send_sem=row_send.at[chunk],
                recv_sem=row_recv.at[chunk],
                device_id=group_device(other),
                device_id_type=MESH,
            ).start()
            return carry

        lax.fori_loop(1, groups // 2 + 1, send, 0)

        def rest():
            lax.fori_loop(groups // 2 + 1, groups, send, 0)
            tile_at(gathered_v, (chunk,), group)[...] = combined(group)

        others[chunk] = rest

    def send_rows(chunk):
        others[chunk]()

    def side_by_side(chunk, start, stop):
        return jnp.concatenate(
            [
                gathered_v[chunk, pl.ds(column, groups, stride=tiles), :]
                for column in range(start, stop)
            ],
            axis=1,
        )

    blocks = groups // 8

    def gram_of(chunk):
        wait_bytes(gathered_v.at[chunk, pl.ds(0, (groups - 1) * tiles)], row_recv.at[chunk])
        pltpu.make_async_copy(gathered_v.at[chunk], gathered.at[chunk], out_sem.at[chunk]).start()
        first = sum(len(widths) for widths in members[:chunk])
        pieces = [jnp.zeros((8, first * groups * blocks), jnp.float32)] if first else []
        for start, stop in spans(chunk):
            vectors = side_by_side(chunk, start, stop)
            gram = lax.dot_general(
                vectors,
                vectors,
                (((1,), (1,)), ((), ())),
                precision=lax.Precision.HIGHEST,
                preferred_element_type=jnp.float32,
            )
            pieces += [gram[top : top + 8] for top in range(0, groups, 8)]
        used = sum(piece.shape[1] for piece in pieces)
        if used < LANES:
            pieces.append(jnp.zeros((8, LANES - used), jnp.float32))
        grams[chunk] = jnp.concatenate(pieces, axis=1)

    def gram_part(_):
        total = grams[0]
        for chunk in range(1, chunks):
            total = total + grams[chunk]
        gram_parts[0, cluster_me] = total
        broadcast(
            0, gram_parts, cluster_size, cluster_me, cluster_device, gram_part_send, gram_part_recv
        )

    def gram_total(_):
        gram_totals[0, group] = collect(0, gram_parts, cluster_size, gram_part_recv)
        broadcast(0, gram_totals, groups, group, group_device, gram_total_send, gram_total_recv)

    def finish(_):
        total = collect(0, gram_totals, groups, gram_total_recv)
        worst = jnp.zeros((1, 1), jnp.float32)
        number = 0
        for chunk in range(chunks):
            for start, stop in spans(chunk):
                gram = jnp.concatenate(
                    [
                        total[:, groups * block : groups * (block + 1)]
                        for block in range(number * blocks, (number + 1) * blocks)
                    ],
                    axis=0,
                )
                coefficients, doubtful = tree_weights(gram)
                vectors = side_by_side(chunk, start, stop)
                outs[number][...] = jnp.sum(coefficients * vectors, axis=0, keepdims=True)
                worst = jnp.maximum(worst, jnp.max(doubtful, axis=0, keepdims=True))
                number += 1
        flag[0] = worst[0, 0]

    bring(0)
    pl.semaphore_wait(barrier, cluster_size + groups - 2)
    steps = {
        "s0": functools.partial(send_half, 0),
        "s1": functools.partial(send_half, 1),
        "b0": bring,
        "r0": half_sum,
        "c0": half_combine,
        "q1": send_quarter,
        "r1": quarter_sum,
        "c1": quarter_combine,
        "w1": send_rows,
        "r2": gram_of,
        "g2": gram_part,
        "u2": gram_total,
        "f2": finish,
    }
    for step in ORDER:
        steps[step[:2]]("ABC".index(step[2]))

    for chunk in range(chunks):
        for part in range(2):
            half_copy(part, chunk).wait_send()
        for part in range(2):
            quarter_copy(part, chunk).wait_send()
        wait_bytes(gathered_v.at[chunk, pl.ds(0, (groups - 1) * tiles)], row_send.at[chunk])
        for slots, size, sent in (
            (half_sums, pair_size, half_sum_send),
            (quarter_sums, cluster_size, quarter_sum_send),
        ):
            wait_bytes(slots.at[chunk, pl.ds(0, size - 1)], sent.at[chunk])
        pltpu.make_async_copy(gathered_v.at[chunk], gathered.at[chunk], out_sem.at[chunk]).wait()
    for slots, size, sent in (
        (gram_parts, cluster_size, gram_part_send),
        (gram_totals, groups, gram_total_send),
    ):
        wait_bytes(slots.at[0, pl.ds(0, size - 1)], sent.at[0])


def level_by_level(vectors):
    while vectors.shape[0] > 1:
        lower, upper = vectors[0::2], vectors[1::2]
        totals = lax.psum(
            jnp.stack(
                [
                    jnp.sum(lower * upper, axis=(1, 2)),
                    jnp.sum(lower * lower, axis=(1, 2)),
                    jnp.sum(upper * upper, axis=(1, 2)),
                ]
            ),
            ("replica", "tensor"),
        )
        low = lower_weight(totals[0], totals[1])[:, None, None]
        up = lower_weight(totals[0], totals[2])[:, None, None]
        vectors = low * lower + up * upper
    return vectors.reshape(1, -1)


def hand_on(*refs):
    for source, target in zip(refs[: len(refs) // 2], refs[len(refs) // 2 :]):
        target[...] = source[...]


def per_device(*grads):
    replicas, tensors = lax.axis_size("replica"), lax.axis_size("tensor")
    groups = replicas // 4
    widths = [member.shape[2] // LANES for member in grads]
    tiles = max(widths)
    members = []
    for width in widths:
        if members and sum(members[-1]) + width <= tiles:
            members[-1].append(width)
        else:
            members.append([width])
    chunks = len(members)
    f32 = jnp.float32
    dma = pltpu.SemaphoreType.DMA
    results = pl.pallas_call(
        functools.partial(kernel, replicas, tensors, members, tiles),
        out_shape=[jax.ShapeDtypeStruct((1, member.shape[2]), f32) for member in grads]
        + [
            jax.ShapeDtypeStruct((chunks, groups * tiles, LANES), f32),
            jax.ShapeDtypeStruct((1,), f32),
        ],
        in_specs=[pl.BlockSpec(memory_space=pl.ANY)] * len(grads),
        out_specs=[pl.BlockSpec(memory_space=pltpu.VMEM)] * len(grads)
        + [pl.BlockSpec(memory_space=pl.ANY), pl.BlockSpec(memory_space=pltpu.SMEM)],
        scratch_shapes=[
            pltpu.VMEM((chunks, replicas, tiles * LANES), f32),
            pltpu.VMEM((chunks, replicas * tiles, LANES), f32),
            pltpu.VMEM((chunks, 2, groups * tiles, LANES), f32),
            pltpu.VMEM((chunks, 2, groups * tiles, LANES), f32),
            pltpu.VMEM((chunks, groups * tiles, LANES), f32),
            pltpu.VMEM((chunks, groups * tiles, LANES), f32),
            pltpu.VMEM((chunks, groups * tiles, LANES), f32),
            pltpu.VMEM((chunks, 8, LANES), f32),
        ]
        + [
            pltpu.VMEM((chunks, size, 1, LANES), f32) for size in (2 * tensors, 4 * tensors)
        ]
        + [pltpu.VMEM((1, size, 8, LANES), f32) for size in (4 * tensors, groups)]
        + [
            dma((len(grads),)),
        ]
        + [dma((chunks, 2))] * 4
        + [dma((chunks,))] * 11,
        compiler_params=pltpu.CompilerParams(
            collective_id=0, has_side_effects=True, vmem_limit_bytes=60 * 1024 * 1024
        ),
    )(*grads)
    combined, gathered, flag = results[: len(grads)], results[len(grads)], results[-1]

    def again(combined, gathered):
        outputs = []
        for chunk, in_chunk in enumerate(members):
            vectors = gathered[chunk].reshape(groups, tiles, LANES)
            start = 0
            for width in in_chunk:
                outputs.append(level_by_level(vectors[:, start : start + width]))
                start += width
        return outputs

    chosen = lax.cond(
        flag[0] > 0.0,
        again,
        lambda combined, gathered: list(combined),
        list(combined),
        gathered,
    )
    return tuple(
        pl.pallas_call(
            hand_on,
            out_shape=[jax.ShapeDtypeStruct(member.shape, f32) for member in chosen],
            in_specs=[pl.BlockSpec(memory_space=pltpu.VMEM)] * len(chosen),
            out_specs=[pl.BlockSpec(memory_space=pltpu.VMEM)] * len(chosen),
        )(*chosen)
    )


def solution(mesh):
    return jax.shard_map(
        per_device,
        mesh=mesh,
        in_specs=(P("replica", None, "tensor"),) * 4,
        out_specs=(P("replica", "tensor"),) * 4,
        check_vma=False,
    )
```

```python
import functools

import jax
import jax.numpy as jnp
from jax import lax
from jax.experimental import pallas as pl
from jax.experimental.pallas import tpu as pltpu
from jax.sharding import PartitionSpec as P

EPSILON = 1e-06
LANES = 128
TRUSTED = 0.03
MESH = pl.DeviceIdType.MESH
ORDER = (
    "s0A", "s1A", "b0B", "s0B", "b0C", "r0A", "s1B", "c0A", "q1A", "r0B", "s0C", "s1C", "r1A",
    "c0B", "q1B", "r0C", "c1A", "r1B", "c0C", "q1C", "w1A", "r1C", "c1B", "w1B", "c1C", "w1C",
    "r2A", "r2B", "r2C", "g2C", "e2C", "u2C", "f2C",
)


def lower_weight(cross, norm):
    return 1.0 - cross / (2.0 * (norm + EPSILON))


def tree_weights(gram):
    count = gram.shape[0]
    across = lax.broadcasted_iota(jnp.int32, (count, count), 1)
    down = lax.broadcasted_iota(jnp.int32, (count, count), 0)
    coefficients = jnp.ones((count, 1), jnp.float32)
    doubtful = jnp.zeros((count, 1), jnp.float32)
    scaled = gram
    for level in range(count.bit_length() - 1):
        same = (across >> level) == (down >> level)
        either = (across >> (level + 1)) == (down >> (level + 1))
        own = jnp.where(same, scaled, 0.0)
        sibling = jnp.where(either, scaled, 0.0) - own
        sizes = jnp.abs(own)

        def column_of(terms):
            partial = jnp.sum(terms, axis=0, keepdims=True)
            return jnp.sum(jnp.where(same, partial, 0.0), axis=1, keepdims=True)

        def row_of(terms):
            partial = jnp.sum(terms, axis=1, keepdims=True)
            return jnp.sum(jnp.where(same, partial, 0.0), axis=0, keepdims=True)

        norm = column_of(own)
        column = lower_weight(column_of(sibling), norm)
        row = lower_weight(row_of(sibling), row_of(own))
        doubtful = jnp.maximum(
            doubtful, jnp.where(norm < TRUSTED * column_of(sizes), 1.0, 0.0)
        )
        coefficients = coefficients * column
        scaled = scaled * column * row
    return coefficients, doubtful


def kernel(
    replicas,
    tensors,
    members,
    tiles,
    *refs,
):
    count = sum(len(chunk) for chunk in members)
    chunks = len(members)
    inputs, outs, rest = refs[:count], refs[count : 2 * count], refs[2 * count :]
    (gathered, flag, raw, laid, half_in, half, quarter_in, quarter, gathered_v, grams,
     half_sums, quarter_sums, gram_parts, gram_totals,
     in_sem, half_send, half_recv, *semaphores) = rest
    (quarter_send, quarter_recv, row_send, row_recv, out_sem,
     half_sum_send, half_sum_recv, quarter_sum_send, quarter_sum_recv,
     gram_part_send, gram_part_recv, gram_total_send, gram_total_recv) = semaphores

    groups = replicas // 4
    replica = lax.axis_index("replica")
    tensor = lax.axis_index("tensor")
    group = replica // 4
    local = replica % 4
    bit = local % 2
    high = local // 2

    pair_me, cluster_me = bit * tensors + tensor, local * tensors + tensor
    pair_size, cluster_size = 2 * tensors, 4 * tensors

    def pair_device(index):
        return (group * 4 + high * 2 + index // tensors, index % tensors)

    def cluster_device(index):
        return (group * 4 + index // tensors, index % tensors)

    def group_device(index):
        return (index * 4 + local, tensor)

    barrier = pltpu.get_barrier_semaphore()

    def greet(size, me, device):
        def one(step, carry):
            pl.semaphore_signal(
                barrier, inc=1, device_id=device((me + step) % size), device_id_type=MESH
            )
            return carry

        lax.fori_loop(1, size, one, 0)


    input_copies = []
    number = 0
    for chunk, widths in enumerate(members):
        start = 0
        for width in widths:
            input_copies.append(
                pltpu.make_async_copy(
                    inputs[number].at[0],
                    raw.at[chunk, :, pl.ds(start, width * LANES)],
                    in_sem.at[number],
                )
            )
            start += width * LANES
            number += 1
    for copy in input_copies:
        copy.start()

    greet(cluster_size, cluster_me, cluster_device)
    greet(groups, group, group_device)

    rows_of_tile = lax.broadcasted_iota(jnp.int32, (tiles, LANES), 0)
    lane = lax.broadcasted_iota(jnp.int32, (1, LANES), 1)

    def spans(chunk):
        start = 0
        for width in members[chunk]:
            yield start, start + width
            start += width

    def bring(chunk):
        first = sum(len(widths) for widths in members[:chunk])
        for number in range(first, first + len(members[chunk])):
            input_copies[number].wait()

        def block(step, carry):
            top = pl.multiple_of(step * 8, 8)
            for column in range(tiles):
                laid[chunk, pl.ds(top * tiles + column, 8, stride=tiles), :] = raw[
                    chunk, pl.ds(top, 8), pl.ds(column * LANES, LANES)
                ]
            return carry

        lax.fori_loop(0, replicas // 8, block, 0)

    def half_copy(part, chunk):
        return pltpu.make_async_remote_copy(
            src_ref=laid.at[chunk].reshape(groups, 4, tiles, LANES).at[:, 1 - bit + 2 * part],
            dst_ref=half_in.at[chunk, part].reshape(groups, tiles, LANES),
            send_sem=half_send.at[chunk, part],
            recv_sem=half_recv.at[chunk, part],
            device_id=(replica + 1 - 2 * bit, tensor),
            device_id_type=MESH,
        )

    def quarter_copy(part, chunk):
        rows = pl.ds(part * (groups // 2) * tiles, groups // 2 * tiles)
        return pltpu.make_async_remote_copy(
            src_ref=half.at[chunk, 1 - high, rows],
            dst_ref=quarter_in.at[chunk, rows],
            send_sem=quarter_send.at[chunk, part],
            recv_sem=quarter_recv.at[chunk, part],
            device_id=(replica + 2 - 4 * high, tensor),
            device_id_type=MESH,
        )

    def broadcast(chunk, slots, size, near, me, device, send_sem, recv_sem):
        def send(index):
            pltpu.make_async_remote_copy(
                src_ref=slots.at[chunk, me],
                dst_ref=slots.at[chunk, me],
                send_sem=send_sem.at[chunk],
                recv_sem=recv_sem.at[chunk],
                device_id=device(index),
                device_id_type=MESH,
            ).start()

        def along_z(step, carry):
            send(((me // near + 1) * near + step) % size)
            return carry

        def at_one_z(step, carry):
            send(me // near * near + (me + step) % near)
            return carry

        lax.fori_loop(0, size - near, along_z, 0)
        lax.fori_loop(1, near, at_one_z, 0)

    def wait_bytes(ref, semaphore):
        pltpu.make_async_copy(ref, ref, semaphore).wait()

    def collect(chunk, slots, size, recv_sem):
        wait_bytes(slots.at[chunk, pl.ds(0, size - 1)], recv_sem.at[chunk])
        total = slots[chunk, 0]
        for index in range(1, size):
            total = total + slots[chunk, index]
        return total

    def tile_at(ref, index, step):
        return ref.at[index + (pl.ds(pl.multiple_of(step * tiles, 8), tiles),)]

    def statistics(chunk, pairs_at, mine_is_low):
        def one(step, carry):
            for own, theirs in pairs_at(step):
                carry = (
                    carry[0] + own * theirs,
                    carry[1] + own * own,
                    carry[2] + theirs * theirs,
                )
            return carry

        zero = jnp.zeros((tiles, LANES), jnp.float32)
        cross, own, theirs = lax.fori_loop(0, groups, one, (zero, zero, zero))
        lower = jnp.where(mine_is_low, own, theirs)
        upper = jnp.where(mine_is_low, theirs, own)
        message = jnp.zeros((1, LANES), jnp.float32)
        place = 0
        for start, stop in spans(chunk):
            inside = (rows_of_tile >= start) & (rows_of_tile < stop)
            for value in (cross, lower, upper):
                total = jnp.sum(jnp.where(inside, value, 0.0), axis=0, keepdims=True)
                total = jnp.sum(total, axis=1, keepdims=True)
                message = jnp.where(lane == place, total, message)
                place += 1
        return message

    def weights(chunk, total, mine_is_low):
        own_weight = jnp.zeros((tiles, LANES), jnp.float32)
        their_weight = jnp.zeros((tiles, LANES), jnp.float32)
        for number, (start, stop) in enumerate(spans(chunk)):
            inside = (rows_of_tile >= start) & (rows_of_tile < stop)
            cross, low_norm, up_norm = (
                total[:, 3 * number + place : 3 * number + place + 1] for place in range(3)
            )
            low = lower_weight(cross, low_norm)
            up = lower_weight(cross, up_norm)
            own_weight = jnp.where(inside, jnp.where(mine_is_low, low, up), own_weight)
            their_weight = jnp.where(inside, jnp.where(mine_is_low, up, low), their_weight)
        return own_weight, their_weight

    def half_pair(chunk, part, step):
        own = tile_at(laid, (chunk,), step * 4 + bit + 2 * part)[...]
        return own, tile_at(half_in, (chunk, part), step)[...]

    def quarter_pair(chunk, step):
        own = tile_at(half, (chunk, high), step)[...]
        return own, tile_at(quarter_in, (chunk,), step)[...]

    kept, others = {}, {}

    def send_half(part, chunk):
        half_copy(part, chunk).start()

    def half_sum(chunk):
        for part in range(2):
            half_copy(part, chunk).wait_recv()
        half_sums[chunk, pair_me] = statistics(
            chunk, lambda step: [half_pair(chunk, part, step) for part in range(2)], bit == 0
        )
        broadcast(chunk, half_sums, pair_size, tensors, pair_me, pair_device, half_sum_send, half_sum_recv)

    def half_combine(chunk):
        total = collect(chunk, half_sums, pair_size, half_sum_recv)
        own_weight, their_weight = weights(chunk, total, bit == 0)

        def combine(part, start, stop):
            def one(step, carry):
                own, theirs = half_pair(chunk, part, step)
                tile_at(half, (chunk, part), step)[...] = own_weight * own + their_weight * theirs
                return carry

            lax.fori_loop(start, stop, one, 0)

        combine(1 - high, 0, groups // 2)
        quarter_copy(0, chunk).start()
        combine(1 - high, groups // 2, groups)
        kept[chunk] = lambda: combine(high, 0, groups)

    def send_quarter(chunk):
        quarter_copy(1, chunk).start()
        kept[chunk]()

    def quarter_sum(chunk):
        for part in range(2):
            quarter_copy(part, chunk).wait_recv()
        quarter_sums[chunk, cluster_me] = statistics(
            chunk, lambda step: [quarter_pair(chunk, step)], high == 0
        )
        broadcast(
            chunk, quarter_sums, cluster_size, tensors, cluster_me, cluster_device, quarter_sum_send, quarter_sum_recv
        )

    def quarter_combine(chunk):
        total = collect(chunk, quarter_sums, cluster_size, quarter_sum_recv)
        own_weight, their_weight = weights(chunk, total, high == 0)

        def combined(index):
            own, theirs = quarter_pair(chunk, index)
            return own_weight * own + their_weight * theirs

        def send(step, carry):
            other = (group + step) % groups
            tile_at(quarter, (chunk,), other)[...] = combined(other)
            pltpu.make_async_remote_copy(
                src_ref=tile_at(quarter, (chunk,), other),
                dst_ref=tile_at(gathered_v, (chunk,), group),
                send_sem=row_send.at[chunk],
                recv_sem=row_recv.at[chunk],
                device_id=group_device(other),
                device_id_type=MESH,
            ).start()
            return carry

        lax.fori_loop(1, groups // 2 + 1, send, 0)

        def rest():
            lax.fori_loop(groups // 2 + 1, groups, send, 0)
            tile_at(gathered_v, (chunk,), group)[...] = combined(group)

        others[chunk] = rest

    def send_rows(chunk):
        others[chunk]()

    def side_by_side(chunk, start, stop):
        return jnp.concatenate(
            [
                gathered_v[chunk, pl.ds(column, groups, stride=tiles), :]
                for column in range(start, stop)
            ],
            axis=1,
        )

    blocks = groups // 8

    def gram_of(chunk):
        wait_bytes(gathered_v.at[chunk, pl.ds(0, (groups - 1) * tiles)], row_recv.at[chunk])
        pltpu.make_async_copy(gathered_v.at[chunk], gathered.at[chunk], out_sem.at[chunk]).start()
        first = sum(len(widths) for widths in members[:chunk])
        pieces = [jnp.zeros((8, first * groups * blocks), jnp.float32)] if first else []
        for start, stop in spans(chunk):
            vectors = side_by_side(chunk, start, stop)
            gram = lax.dot_general(
                vectors,
                vectors,
                (((1,), (1,)), ((), ())),
                precision=lax.Precision.HIGHEST,
                preferred_element_type=jnp.float32,
            )
            pieces += [gram[top : top + 8] for top in range(0, groups, 8)]
        used = sum(piece.shape[1] for piece in pieces)
        if used < LANES:
            pieces.append(jnp.zeros((8, LANES - used), jnp.float32))
        grams[chunk] = jnp.concatenate(pieces, axis=1)

    def gram_part(_):
        total = grams[0]
        for chunk in range(1, chunks):
            total = total + grams[chunk]
        gram_parts[0, cluster_me] = total
        broadcast(
            0, gram_parts, cluster_size, tensors, cluster_me, cluster_device, gram_part_send, gram_part_recv
        )

    def settle(_):
        for chunk in range(chunks):
            for part in range(2):
                half_copy(part, chunk).wait_send()
            for part in range(2):
                quarter_copy(part, chunk).wait_send()
            wait_bytes(gathered_v.at[chunk, pl.ds(0, (groups - 1) * tiles)], row_send.at[chunk])
            for slots, size, sent in (
                (half_sums, pair_size, half_sum_send),
                (quarter_sums, cluster_size, quarter_sum_send),
            ):
                wait_bytes(slots.at[chunk, pl.ds(0, size - 1)], sent.at[chunk])
            pltpu.make_async_copy(gathered_v.at[chunk], gathered.at[chunk], out_sem.at[chunk]).wait()

    def gram_total(_):
        gram_totals[0, group] = collect(0, gram_parts, cluster_size, gram_part_recv)
        broadcast(0, gram_totals, groups, 1, group, group_device, gram_total_send, gram_total_recv)

    def finish(_):
        total = collect(0, gram_totals, groups, gram_total_recv)
        worst = jnp.zeros((1, 1), jnp.float32)
        number = 0
        for chunk in range(chunks):
            for start, stop in spans(chunk):
                gram = jnp.concatenate(
                    [
                        total[:, groups * block : groups * (block + 1)]
                        for block in range(number * blocks, (number + 1) * blocks)
                    ],
                    axis=0,
                )
                coefficients, doubtful = tree_weights(gram)
                vectors = side_by_side(chunk, start, stop)
                outs[number][...] = jnp.sum(coefficients * vectors, axis=0, keepdims=True)
                worst = jnp.maximum(worst, jnp.max(doubtful, axis=0, keepdims=True))
                number += 1
        flag[0] = worst[0, 0]

    bring(0)
    pl.semaphore_wait(barrier, cluster_size + groups - 2)
    steps = {
        "s0": functools.partial(send_half, 0),
        "s1": functools.partial(send_half, 1),
        "b0": bring,
        "r0": half_sum,
        "c0": half_combine,
        "q1": send_quarter,
        "r1": quarter_sum,
        "c1": quarter_combine,
        "w1": send_rows,
        "r2": gram_of,
        "g2": gram_part,
        "e2": settle,
        "u2": gram_total,
        "f2": finish,
    }
    for step in ORDER:
        steps[step[:2]]("ABC".index(step[2]))

    for slots, size, sent in (
        (gram_parts, cluster_size, gram_part_send),
        (gram_totals, groups, gram_total_send),
    ):
        wait_bytes(slots.at[0, pl.ds(0, size - 1)], sent.at[0])


def level_by_level(vectors):
    while vectors.shape[0] > 1:
        lower, upper = vectors[0::2], vectors[1::2]
        totals = lax.psum(
            jnp.stack(
                [
                    jnp.sum(lower * upper, axis=(1, 2)),
                    jnp.sum(lower * lower, axis=(1, 2)),
                    jnp.sum(upper * upper, axis=(1, 2)),
                ]
            ),
            ("replica", "tensor"),
        )
        low = lower_weight(totals[0], totals[1])[:, None, None]
        up = lower_weight(totals[0], totals[2])[:, None, None]
        vectors = low * lower + up * upper
    return vectors.reshape(1, -1)


def hand_on(*refs):
    for source, target in zip(refs[: len(refs) // 2], refs[len(refs) // 2 :]):
        target[...] = source[...]


def per_device(*grads):
    replicas, tensors = lax.axis_size("replica"), lax.axis_size("tensor")
    groups = replicas // 4
    widths = [member.shape[2] // LANES for member in grads]
    tiles = max(widths)
    members = []
    for width in widths:
        if members and sum(members[-1]) + width <= tiles:
            members[-1].append(width)
        else:
            members.append([width])
    chunks = len(members)
    f32 = jnp.float32
    dma = pltpu.SemaphoreType.DMA
    results = pl.pallas_call(
        functools.partial(kernel, replicas, tensors, members, tiles),
        out_shape=[jax.ShapeDtypeStruct((1, member.shape[2]), f32) for member in grads]
        + [
            jax.ShapeDtypeStruct((chunks, groups * tiles, LANES), f32),
            jax.ShapeDtypeStruct((1,), f32),
        ],
        in_specs=[pl.BlockSpec(memory_space=pl.ANY)] * len(grads),
        out_specs=[pl.BlockSpec(memory_space=pltpu.VMEM)] * len(grads)
        + [pl.BlockSpec(memory_space=pl.ANY), pl.BlockSpec(memory_space=pltpu.SMEM)],
        scratch_shapes=[
            pltpu.VMEM((chunks, replicas, tiles * LANES), f32),
            pltpu.VMEM((chunks, replicas * tiles, LANES), f32),
            pltpu.VMEM((chunks, 2, groups * tiles, LANES), f32),
            pltpu.VMEM((chunks, 2, groups * tiles, LANES), f32),
            pltpu.VMEM((chunks, groups * tiles, LANES), f32),
            pltpu.VMEM((chunks, groups * tiles, LANES), f32),
            pltpu.VMEM((chunks, groups * tiles, LANES), f32),
            pltpu.VMEM((chunks, 8, LANES), f32),
        ]
        + [
            pltpu.VMEM((chunks, size, 1, LANES), f32) for size in (2 * tensors, 4 * tensors)
        ]
        + [pltpu.VMEM((1, size, 8, LANES), f32) for size in (4 * tensors, groups)]
        + [
            dma((len(grads),)),
        ]
        + [dma((chunks, 2))] * 4
        + [dma((chunks,))] * 11,
        compiler_params=pltpu.CompilerParams(
            collective_id=0, has_side_effects=True, vmem_limit_bytes=60 * 1024 * 1024
        ),
    )(*grads)
    combined, gathered, flag = results[: len(grads)], results[len(grads)], results[-1]

    def again(combined, gathered):
        outputs = []
        for chunk, in_chunk in enumerate(members):
            vectors = gathered[chunk].reshape(groups, tiles, LANES)
            start = 0
            for width in in_chunk:
                outputs.append(level_by_level(vectors[:, start : start + width]))
                start += width
        return outputs

    chosen = lax.cond(
        flag[0] > 0.0,
        again,
        lambda combined, gathered: list(combined),
        list(combined),
        gathered,
    )
    return tuple(
        pl.pallas_call(
            hand_on,
            out_shape=[jax.ShapeDtypeStruct(member.shape, f32) for member in chosen],
            in_specs=[pl.BlockSpec(memory_space=pltpu.VMEM)] * len(chosen),
            out_specs=[pl.BlockSpec(memory_space=pltpu.VMEM)] * len(chosen),
        )(*chosen)
    )


def solution(mesh):
    return jax.shard_map(
        per_device,
        mesh=mesh,
        in_specs=(P("replica", None, "tensor"),) * 4,
        out_specs=(P("replica", "tensor"),) * 4,
        check_vma=False,
    )
```
